32 devices in a mesh: pair: 8 (over y, x, core), lam: 4 (over z).
Axes of the slice: x: 2, y: 2, z: 4, core: 2. Of those that a mesh axis runs over, the one named last changes fastest.
Arguments:
- integrals: bfloat16 [8, 32, 4, 64, 1024], P('pair', 'lam'), may hold values from -0.119628906 to 0.119628906
- tile_pair: int32 [8, 32], P('pair', 'lam'), may hold values from 0 to 15, as said below
- tile_lam: int32 [8, 32], P('pair', 'lam'), may hold values from 0 to 15, as said below
- tile_count: int32 [8, 4], P('pair', 'lam'), may hold values from 1 to 8, as said below
- mu_index: int32 [512], P('pair'), may hold values from 0 to 1023
- nu_index: int32 [512], P('pair'), may hold values from 0 to 1023
- occupied_coef: bfloat16 [1024, 16], replicated, may hold values from -1.5 to 1.5
- virtual_coef: bfloat16 [1024, 1280], replicated, may hold values from -1.5 to 1.5
Outputs:
- orbital_integrals: float32 [16, 1280, 20480], P('lam', 'pair')
The draws below stay inside these ranges and needn't reach their ends.
Inputs may be any that keep to these rules, and one draw needn't show every extreme that they name: On every device the live and dead slots name distinct pairs of (tile_pair, tile_lam); tile_pair lies in 0 to 15. On lam index l every slot's tile_lam lies in l * 4 to (l + 1) * 4 - 1. Slots from tile_count on are dead and their integrals are ignored; some device has all 8 slots live.
All inputs are finite; a program needn't handle non-finite values.
Results may differ from the reference program's by a relative error of at most 0.0049.
Values may be sent and summed in bfloat16 or wider, within the bound.
A program may use at most 128 MiB of HBM per device.

```python
import jax
import jax.numpy as jnp
from jax import lax

NBF = 1024
OCC = 16
VIR = 1280
BLK = 64
PROWS = 4
TILE_CAP = 8
PB_DEV = 16
PAIR_SHARDS = 8
LAM_SHARDS = 4
LB_DEV = 4
PAIRS = 512


def tile_lists(key):
    list_key = jax.random.fold_in(key, 11)
    device_keys = jax.random.split(list_key, PAIR_SHARDS * LAM_SHARDS)

    def one_device(device_key):
        chosen = jax.random.permutation(device_key, PB_DEV * LB_DEV)[:TILE_CAP]
        return (chosen // LB_DEV, chosen % LB_DEV)
    pair_blocks, lam_offsets = jax.vmap(one_device)(device_keys)
    pair_blocks = pair_blocks.reshape(PAIR_SHARDS, LAM_SHARDS, TILE_CAP)
    lam_offsets = lam_offsets.reshape(PAIR_SHARDS, LAM_SHARDS, TILE_CAP)
    lam_base = jnp.arange(LAM_SHARDS, dtype=jnp.int32).reshape(1, LAM_SHARDS, 1) * LB_DEV
    lam_blocks = lam_offsets + lam_base
    pair_out = pair_blocks.reshape(PAIR_SHARDS, LAM_SHARDS * TILE_CAP).astype(jnp.int32)
    lam_out = lam_blocks.reshape(PAIR_SHARDS, LAM_SHARDS * TILE_CAP).astype(jnp.int32)
    return (pair_out, lam_out)


def draw_tile_pair(key, part):
    return tile_lists(key)[0]


def draw_tile_lam(key, part):
    return tile_lists(key)[1]


def draw_tile_count(key, part):
    counts = jax.random.randint(jax.random.fold_in(key, 23), (PAIR_SHARDS * LAM_SHARDS,), 1, TILE_CAP + 1)
    busiest = jax.random.randint(jax.random.fold_in(key, 29), (), 0, PAIR_SHARDS * LAM_SHARDS)
    counts = jnp.where(jnp.arange(PAIR_SHARDS * LAM_SHARDS) == busiest, TILE_CAP, counts)
    return counts.reshape(PAIR_SHARDS, LAM_SHARDS).astype(jnp.int32)


def set_ends(values, own_key, low, high):
    index_at = [jax.random.randint(jax.random.fold_in(own_key, axis), (), 0, length) for axis, length in enumerate(values.shape)]
    main_axis = values.shape.index(max(values.shape))
    next_to = index_at[:main_axis] + [(index_at[main_axis] + 1) % values.shape[main_axis]] + index_at[main_axis + 1:]
    return values.at[tuple(index_at)].set(low).at[tuple(next_to)].set(high)


def levels(key, dims, shards, low, largest):
    gain, own = 1.0, jax.random.fold_in(key, 6)
    for position, parts in shards:
        steps = jnp.exp(jax.random.uniform(jax.random.fold_in(own, position), (parts,), jnp.float32, low / len(shards), largest / len(shards)))
        gain = gain * jnp.repeat(steps, dims[position] // parts).reshape([-1 if axis == position else 1 for axis in range(len(dims))])
    return gain


def gaussian(rng, shape, spread, bound, cuts=(), kind=jnp.bfloat16):
    gain = levels(rng, shape, cuts, -0.22, 0.18) if cuts else 1.0
    drawn = jax.random.normal(rng, shape, jnp.float32) * spread * gain
    return jnp.minimum(jnp.maximum(drawn, -bound), bound).astype(kind)


def setup_inputs(seed: int = 0) -> dict:
    keys = jax.random.split(jax.random.key(seed), 9)
    return {
        "integrals": gaussian(keys[0], (PAIR_SHARDS, LAM_SHARDS * TILE_CAP, PROWS, BLK, NBF), 0.02, 0.119628906, ((0, 8), (1, 4))),
        "tile_pair": draw_tile_pair(jax.random.fold_in(keys[8], 71), 0),
        "tile_lam": draw_tile_lam(jax.random.fold_in(keys[8], 71), 0),
        "tile_count": draw_tile_count(jax.random.fold_in(keys[8], 71), 0),
        "mu_index": set_ends(jax.random.randint(keys[4], (PAIRS,), 0, NBF), jax.random.fold_in(keys[4], 1), 0, NBF - 1).astype(jnp.int32),
        "nu_index": set_ends(jax.random.randint(keys[5], (PAIRS,), 0, NBF), jax.random.fold_in(keys[5], 1), 0, NBF - 1).astype(jnp.int32),
        "occupied_coef": gaussian(keys[6], (NBF, OCC), 0.25, 1.5),
        "virtual_coef": gaussian(keys[7], (NBF, VIR), 0.25, 1.5),
    }


def shard_mixed(shard, integrals, tile_pair, tile_lam, tile_count, occ_wide, virtual_coef):
    pair_rows = PB_DEV * PROWS
    tile_data = integrals[shard]
    pair_list = tile_pair[shard]
    lam_list = tile_lam[shard]
    live_counts = tile_count[shard]

    def add_tile(partial_value, slot_index):
        device_slot = slot_index % TILE_CAP
        owner_lam = slot_index // TILE_CAP
        is_live = (device_slot < live_counts[owner_lam]).astype(jnp.float32)
        occ_rows = lax.dynamic_slice_in_dim(occ_wide, (lam_list[slot_index] * BLK).astype(jnp.int32), BLK, 0)
        contrib = jnp.einsum("rls,lj->jrs", tile_data[slot_index].astype(jnp.float32), occ_rows, precision=lax.Precision.HIGHEST)
        row_start = (pair_list[slot_index] * PROWS).astype(jnp.int32)
        current = lax.dynamic_slice_in_dim(partial_value, row_start, PROWS, 1)
        return lax.dynamic_update_slice_in_dim(partial_value, current + is_live * contrib, row_start, 1), None

    start_half = jnp.zeros((OCC, pair_rows, NBF), jnp.float32)
    half, _ = lax.scan(add_tile, start_half, jnp.arange(LAM_SHARDS * TILE_CAP, dtype=jnp.int32))
    half_low = half.astype(jnp.bfloat16)
    mixed = jnp.dot(half_low.reshape(OCC * pair_rows, NBF), virtual_coef, preferred_element_type=jnp.float32)
    return mixed.reshape(OCC, pair_rows, VIR).astype(jnp.bfloat16)


def reference(integrals, tile_pair, tile_lam, tile_count, mu_index, nu_index, occupied_coef, virtual_coef):
    occ_wide = occupied_coef.astype(jnp.float32)
    vir_wide = virtual_coef.astype(jnp.float32)
    pair_rows = PB_DEV * PROWS

    def add_shard(running, shard):
        mixed = shard_mixed(shard, integrals, tile_pair, tile_lam, tile_count, occ_wide, virtual_coef)
        mixed = lax.optimization_barrier(mixed).astype(jnp.float32)
        row_start = (shard * pair_rows).astype(jnp.int32)
        first_rows = lax.dynamic_slice_in_dim(mu_index, row_start, pair_rows)
        second_rows = lax.dynamic_slice_in_dim(nu_index, row_start, pair_rows)
        weights = (occ_wide[first_rows][:, :, None] * vir_wide[second_rows][:, None, :]).astype(jnp.bfloat16)
        weights = lax.optimization_barrier(weights).astype(jnp.float32).reshape(pair_rows, OCC * VIR)
        mixed_rows = jnp.transpose(mixed, (0, 2, 1)).reshape(OCC * VIR, pair_rows)
        return running + jnp.dot(mixed_rows, weights, precision=lax.Precision.HIGHEST), None

    start_total = jnp.zeros((OCC * VIR, OCC * VIR), jnp.float32)
    total, _ = lax.scan(add_shard, start_total, jnp.arange(PAIR_SHARDS, dtype=jnp.int32))
    return total.reshape(OCC, VIR, OCC * VIR)
```

```python
import functools

import jax
import jax.numpy as jnp
from jax import lax
from jax.experimental import pallas as pl
from jax.experimental.pallas import tpu as pltpu
from jax.sharding import PartitionSpec as P

LANES = 128
ROW_TILE = 16
VMEM_BYTES = 50 * 1024 * 1024
MESH = pl.DeviceIdType.MESH


def round_up(value, step):
    return (value + step - 1) // step * step


def exchange_kernel(
    lam_n, pair_n, chunks, share, share_pad, rows,
    tiles_ref, spread_ref, place_ref, index_ref, occ_ref, vir_ref,
    lhs_ref, occ_rows_ref, vir_rows_ref,
    tile_buf, vir_buf, half_send, half_held, place_held, index_held, pick, mixed_t, mix_send, mix_held,
    tile_sem, vir_sem, place_ssem, place_rsem, index_ssem, index_rsem,
    half_ssem, half_rsem, mix_ssem, mix_rsem,
):
    lam_me = lax.axis_index("lam")
    pair_me = lax.axis_index("pair")
    groups = tile_buf.shape[0]
    depth = tile_buf.shape[1]
    basis = vir_buf.shape[0]

    barrier = pltpu.get_barrier_semaphore()
    for d in range(1, lam_n):
        pl.semaphore_signal(barrier, inc=1, device_id={"lam": lax.rem(lam_me + d, lam_n)}, device_id_type=MESH)
    for d in range(1, pair_n):
        pl.semaphore_signal(barrier, inc=1, device_id={"pair": lax.rem(pair_me + d, pair_n)}, device_id_type=MESH)

    tile_copies = [
        pltpu.make_async_copy(tiles_ref.at[pl.ds(q * depth, depth)], tile_buf.at[q], tile_sem.at[q])
        for q in range(groups)
    ]
    vir_copy = pltpu.make_async_copy(vir_ref, vir_buf, vir_sem)
    for copy in tile_copies:
        copy.start()
    vir_copy.start()

    for q in range(groups):
        tile_copies[q].wait()
        part = jnp.dot(spread_ref[q], tile_buf[q], preferred_element_type=jnp.float32).astype(jnp.bfloat16)
        for g in range(lam_n * chunks):
            half_send[g // chunks, g % chunks, q * ROW_TILE:(q + 1) * ROW_TILE, :] = part[
                g * ROW_TILE:(g + 1) * ROW_TILE
            ]

    pl.semaphore_wait(barrier, lam_n + pair_n - 2)

    sends = []
    place_copies, index_copies, half_copies, mix_copies = [], [], [], []
    for d in range(1, lam_n):
        peer = lax.rem(lam_me + d, lam_n)
        copy = pltpu.make_async_remote_copy(
            src_ref=place_ref, dst_ref=place_held.at[lam_me],
            send_sem=place_ssem.at[d], recv_sem=place_rsem.at[d],
            device_id={"lam": peer}, device_id_type=MESH,
        )
        copy.start()
        place_copies.append(copy)
    for d in range(1, pair_n):
        peer = lax.rem(pair_me + d, pair_n)
        copy = pltpu.make_async_remote_copy(
            src_ref=index_ref, dst_ref=index_held.at[pair_me],
            send_sem=index_ssem.at[d], recv_sem=index_rsem.at[d],
            device_id={"pair": peer}, device_id_type=MESH,
        )
        copy.start()
        index_copies.append(copy)
    for c in range(chunks):
        row_copies = []
        for d in range(1, lam_n):
            peer = lax.rem(lam_me + d, lam_n)
            copy = pltpu.make_async_remote_copy(
                src_ref=half_send.at[peer, c], dst_ref=half_held.at[c, lam_me],
                send_sem=half_ssem.at[c, d], recv_sem=half_rsem.at[c, d],
                device_id={"lam": peer}, device_id_type=MESH,
            )
            copy.start()
            row_copies.append(copy)
        half_copies.append(row_copies)

    place_held[lam_me] = place_ref[...]
    index_held[pair_me] = index_ref[...]
    for c in range(chunks):
        half_held[c, lam_me] = half_send[lam_me, c]

    for copy in index_copies:
        copy.wait_recv()
    for p in range(pair_n):
        line = index_held[p, 0:1, :].astype(jnp.float32)
        column = jnp.transpose(jnp.broadcast_to(line, (LANES, LANES)))
        for b in range(basis // LANES):
            name = (lax.broadcasted_iota(jnp.int32, (LANES, LANES), 1) + b * LANES).astype(jnp.float32)
            hit = jnp.where(column == name, 1.0, 0.0).astype(jnp.bfloat16)
            pick[0, p * rows:(p + 1) * rows, b * LANES:(b + 1) * LANES] = hit[:rows]
            pick[1, p * rows:(p + 1) * rows, b * LANES:(b + 1) * LANES] = hit[rows:]
    occ_rows_ref[...] = jnp.dot(pick[0], occ_ref[...], preferred_element_type=jnp.float32).astype(jnp.bfloat16)
    vir_copy.wait()
    step = 2 * LANES
    for n in range(0, vir_buf.shape[1], step):
        vir_rows_ref[:, n:n + step] = jnp.dot(
            pick[1], vir_buf[:, n:n + step], preferred_element_type=jnp.float32
        ).astype(jnp.bfloat16)

    for copy in place_copies:
        copy.wait_recv()
    place = jnp.transpose(place_held[...].reshape(-1, LANES).astype(jnp.float32)).astype(jnp.bfloat16)

    for c in range(chunks):
        for copy in half_copies[c]:
            copy.wait_recv()
        slots = half_held[c].reshape(-1, basis)
        half_low = jnp.dot(place, slots, preferred_element_type=jnp.float32).astype(jnp.bfloat16)
        for n in range(0, vir_buf.shape[1], step):
            mixed = jnp.dot(half_low, vir_buf[:, n:n + step], preferred_element_type=jnp.float32)
            mixed_t[n:n + step, :] = jnp.transpose(mixed)
        for p in range(pair_n):
            block = mixed_t[p * share:(p + 1) * share, :]
            if share_pad > share:
                block = jnp.concatenate([block, jnp.zeros((share_pad - share, LANES), jnp.float32)], axis=0)
            mix_send[c, p] = block.astype(jnp.bfloat16)
        row_copies = []
        for d in range(1, pair_n):
            peer = lax.rem(pair_me + d, pair_n)
            copy = pltpu.make_async_remote_copy(
                src_ref=mix_send.at[c, peer], dst_ref=mix_held.at[c, pair_me],
                send_sem=mix_ssem.at[c, d], recv_sem=mix_rsem.at[c, d],
                device_id={"pair": peer}, device_id_type=MESH,
            )
            copy.start()
            row_copies.append(copy)
        mix_copies.append(row_copies)
        mix_held[c, pair_me] = mix_send[c, pair_me]

    low_lanes = lax.broadcasted_iota(jnp.int32, (share_pad, LANES), 1) < rows
    for c in range(chunks):
        for copy in mix_copies[c]:
            copy.wait_recv()
        for pp in range(pair_n // 2):
            even = mix_held[c, 2 * pp].astype(jnp.float32)
            odd = mix_held[c, 2 * pp + 1].astype(jnp.float32)
            first = jnp.where(low_lanes, even, pltpu.roll(odd, rows, 1))
            second = jnp.where(low_lanes, pltpu.roll(even, rows, 1), odd)
            lhs_ref[2 * c, :, pp * LANES:(pp + 1) * LANES] = first.astype(jnp.bfloat16)
            lhs_ref[2 * c + 1, :, pp * LANES:(pp + 1) * LANES] = second.astype(jnp.bfloat16)

    for copy in place_copies + index_copies + sum(half_copies, []) + sum(mix_copies, []):
        copy.wait_send()


def product_kernel(share, lhs_ref, occ_rows_ref, vir_rows_ref, out_ref):
    step_i = pl.program_id(0)
    occ_total = occ_rows_ref.shape[1]
    items, share_pad, total_rows = lhs_ref.shape
    ones = lax.broadcasted_iota(jnp.int32, (occ_total, 2 * LANES), 0) == step_i
    chosen = jnp.where(ones, 1.0, 0.0).astype(jnp.bfloat16)
    occ_wide = jnp.dot(occ_rows_ref[...], chosen, preferred_element_type=jnp.float32).astype(jnp.bfloat16)
    lhs = lhs_ref[...].reshape(items * share_pad, total_rows)
    step = 2 * LANES
    for n in range(0, vir_rows_ref.shape[1], step):
        weights = occ_wide * vir_rows_ref[:, n:n + step]
        block = jnp.dot(lhs, weights, preferred_element_type=jnp.float32)
        for j in range(items):
            out_ref[j, :, n:n + step] = block[j * share_pad:j * share_pad + share]


def on_device(
    integrals, tile_pair, tile_lam, tile_count, mu_index, nu_index, occupied_coef, virtual_coef
):
    lam_n = lax.axis_size("lam")
    pair_n = lax.axis_size("pair")
    basis, occ_total = occupied_coef.shape
    vir_total = virtual_coef.shape[1]
    rows = mu_index.shape[0]
    slots, prows, blk = integrals.shape[1:4]
    bf16 = jnp.bfloat16
    both = LANES // rows
    occ_share = occ_total // lam_n
    chunks = occ_share // both
    share = vir_total // pair_n
    share_pad = round_up(share, ROW_TILE)
    duo = ROW_TILE // (both * prows)
    groups = slots // duo
    total_rows = rows * pair_n

    live = jnp.arange(slots, dtype=jnp.int32) < tile_count[0, 0]
    chosen = (tile_lam[0][:, None] == jnp.arange(basis // blk, dtype=jnp.int32)) & live[:, None]
    occ_tiles = jnp.einsum(
        "tl,lmj->tjm", chosen.astype(bf16), occupied_coef.reshape(basis // blk, blk, occ_total),
        preferred_element_type=jnp.float32,
    ).astype(bf16)
    factor = occ_tiles.reshape(groups, duo, lam_n * chunks, both, blk).transpose(0, 2, 3, 1, 4)
    same = (
        jnp.eye(duo, dtype=bool)[:, None, None, :, None] & jnp.eye(prows, dtype=bool)[None, None, :, None, :]
    )
    spread = jnp.where(
        same[None, None, :, :, :, :, :, None],
        factor[:, :, None, :, None, :, None, :],
        jnp.zeros((), bf16),
    ).reshape(groups, lam_n * chunks * ROW_TILE, duo * prows * blk)

    target = tile_pair[0][:, None] * prows + jnp.arange(prows, dtype=jnp.int32)
    hit = (target[:, None, :, None, None] == jnp.arange(rows, dtype=jnp.int32)) & jnp.eye(both, dtype=bool)[
        None, :, None, :, None
    ]
    place = hit.astype(bf16).reshape(slots * both * prows, LANES)
    index = jnp.broadcast_to(jnp.concatenate([mu_index, nu_index])[None, :], (8, 2 * rows))

    vmem = pl.BlockSpec(memory_space=pltpu.VMEM)
    hbm = pl.BlockSpec(memory_space=pl.ANY)
    dma = pltpu.SemaphoreType.DMA
    chunk_rows = slots * both * prows
    lhs, occ_rows, vir_rows = pl.pallas_call(
        functools.partial(exchange_kernel, lam_n, pair_n, chunks, share, share_pad, rows),
        out_shape=(
            jax.ShapeDtypeStruct((occ_share, share_pad, total_rows), bf16),
            jax.ShapeDtypeStruct((total_rows, occ_total), bf16),
            jax.ShapeDtypeStruct((total_rows, vir_total), bf16),
        ),
        in_specs=[hbm, vmem, vmem, vmem, vmem, hbm],
        out_specs=(vmem, vmem, vmem),
        scratch_shapes=[
            pltpu.VMEM((groups, duo * prows * blk, basis), bf16),
            pltpu.VMEM((basis, vir_total), bf16),
            pltpu.VMEM((lam_n, chunks, chunk_rows, basis), bf16),
            pltpu.VMEM((chunks, lam_n, chunk_rows, basis), bf16),
            pltpu.VMEM((lam_n, chunk_rows, LANES), bf16),
            pltpu.VMEM((pair_n, 8, LANES), jnp.int32),
            pltpu.VMEM((2, total_rows, basis), bf16),
            pltpu.VMEM((vir_total, LANES), jnp.float32),
            pltpu.VMEM((chunks, pair_n, share_pad, LANES), bf16),
            pltpu.VMEM((chunks, pair_n, share_pad, LANES), bf16),
            dma((groups,)),
            dma,
            dma((lam_n,)),
            dma((lam_n,)),
            dma((pair_n,)),
            dma((pair_n,)),
            dma((chunks, lam_n)),
            dma((chunks, lam_n)),
            dma((chunks, pair_n)),
            dma((chunks, pair_n)),
        ],
        compiler_params=pltpu.CompilerParams(
            collective_id=0, has_side_effects=True, vmem_limit_bytes=VMEM_BYTES
        ),
        name="exchange",
    )(integrals.reshape(slots * prows * blk, basis), spread, place, index, occupied_coef, virtual_coef)

    return pl.pallas_call(
        functools.partial(product_kernel, share),
        out_shape=jax.ShapeDtypeStruct((occ_share, share, occ_total * vir_total), jnp.float32),
        grid=(occ_total,),
        in_specs=[
            pl.BlockSpec((occ_share, share_pad, total_rows), lambda i: (0, 0, 0)),
            pl.BlockSpec((total_rows, occ_total), lambda i: (0, 0)),
            pl.BlockSpec((total_rows, vir_total), lambda i: (0, 0)),
        ],
        out_specs=pl.BlockSpec((occ_share, share, vir_total), lambda i: (0, 0, i)),
        compiler_params=pltpu.CompilerParams(vmem_limit_bytes=VMEM_BYTES),
        name="product",
    )(lhs, occ_rows, vir_rows)


def solution(mesh):
    placed = (
        P("pair", "lam", None, None, None),
        P("pair", "lam"),
        P("pair", "lam"),
        P("pair", "lam"),
        P("pair"),
        P("pair"),
        P(),
        P(),
    )
    return jax.shard_map(
        on_device, mesh=mesh, in_specs=placed, out_specs=P("lam", "pair", None), check_vma=False
    )
```

```python
import functools

import jax
import jax.numpy as jnp
from jax import lax
from jax.experimental import pallas as pl
from jax.experimental.pallas import tpu as pltpu
from jax.sharding import PartitionSpec as P

LANES = 128
ROW_TILE = 16
VMEM_BYTES = 50 * 1024 * 1024
MESH = pl.DeviceIdType.MESH


def round_up(value, step):
    return (value + step - 1) // step * step


def bits_of(size):
    return size.bit_length() - 1


def split_iota(shape, dim, *sizes):
    left = lax.broadcasted_iota(jnp.int32, shape, dim)
    parts = []
    for size in reversed(sizes):
        parts.append(left & (size - 1))
        left = left >> bits_of(size)
    return [left] + parts[::-1]


def one_hot(hit):
    return jnp.where(hit, 1.0, 0.0).astype(jnp.bfloat16)


def exchange_kernel(
    lam_n, pair_n, chunks, share, share_pad, rows, prows, blk,
    tiles_ref, pair_ref, lam_ref, count_ref, mu_ref, nu_ref, occ_ref, vir_ref,
    lhs_ref, occ_wide_ref, vir_rows_ref,
    tile_buf, vir_buf, place_ref, index_ref, half_send, half_held, place_held, index_held, pick, mixed_t,
    mix_send, mix_held,
    tile_sem, vir_sem, place_ssem, place_rsem, index_ssem, index_rsem,
    half_ssem, half_rsem, mix_ssem, mix_rsem,
):
    lam_me = lax.axis_index("lam")
    pair_me = lax.axis_index("pair")
    groups = tile_buf.shape[0]
    depth = tile_buf.shape[1]
    basis = vir_buf.shape[0]
    occ_total = occ_ref.shape[0]
    both = LANES // rows
    slots = pair_ref.shape[1]
    duo = slots // groups

    barrier = pltpu.get_barrier_semaphore()
    for d in range(1, lam_n):
        pl.semaphore_signal(barrier, inc=1, device_id={"lam": lax.rem(lam_me + d, lam_n)}, device_id_type=MESH)
    for d in range(1, pair_n):
        pl.semaphore_signal(barrier, inc=1, device_id={"pair": lax.rem(pair_me + d, pair_n)}, device_id_type=MESH)

    tile_copies = [
        pltpu.make_async_copy(tiles_ref.at[pl.ds(q * depth, depth)], tile_buf.at[q], tile_sem.at[q])
        for q in range(groups)
    ]
    vir_copy = pltpu.make_async_copy(vir_ref, vir_buf, vir_sem)
    for copy in tile_copies:
        copy.start()
    vir_copy.start()

    slot, row_j, row_k = split_iota((slots * both * prows, LANES), 0, both, prows)
    lane_j, lane_r = split_iota((slots * both * prows, LANES), 1, rows)
    goal = jnp.zeros_like(slot)
    for t in range(slots):
        goal = jnp.where(slot == t, pair_ref[0, t], goal)
    place_ref[...] = one_hot((row_j == lane_j) & (lane_r == goal * prows + row_k))
    index_ref[...] = jnp.zeros_like(index_ref)
    index_ref[0:1, 0:rows] = mu_ref[...]
    index_ref[1:2, 0:rows] = nu_ref[...]

    lam_rows = basis // lam_n
    width = slots * prows * blk
    lane_t, _, lane_m = split_iota((1, width), 1, prows, blk)
    source = jnp.zeros_like(lane_t)
    for t in range(slots):
        first = jnp.where(count_ref[0, 0] > t, lam_ref[0, t] * blk - lam_me * lam_rows, -2 * basis)
        source = jnp.where(lane_t == t, first, source)
    source = source + lane_m
    chosen = one_hot(lax.broadcasted_iota(jnp.int32, (lam_rows, width), 0) == source)
    occ_own = occ_ref[:, pl.ds(pl.multiple_of(lam_me * lam_rows, lam_rows), lam_rows)]
    occ_tiles = jnp.dot(occ_own, chosen, preferred_element_type=jnp.float32).astype(jnp.bfloat16)
    height = lam_n * chunks * ROW_TILE
    group, _, repeat_j, _ = split_iota((height, occ_total), 0, duo, both, prows)
    repeat = one_hot(lax.broadcasted_iota(jnp.int32, (height, occ_total), 1) == group * both + repeat_j)
    factor = jnp.dot(repeat, occ_tiles, preferred_element_type=jnp.float32)
    _, row_t, _, row_k = split_iota((height, width), 0, duo, both, prows)
    lane_t, lane_k, _ = split_iota((height, width), 1, prows, blk)
    spread = jnp.where((row_t == (lane_t & (duo - 1))) & (row_k == lane_k), factor, 0.0).astype(jnp.bfloat16)

    for q in range(groups):
        tile_copies[q].wait()
        part = jnp.dot(
            spread[:, q * depth:(q + 1) * depth], tile_buf[q], preferred_element_type=jnp.float32
        ).astype(jnp.bfloat16)
        for g in range(lam_n * chunks):
            half_send[g // chunks, g % chunks, q * ROW_TILE:(q + 1) * ROW_TILE, :] = part[
                g * ROW_TILE:(g + 1) * ROW_TILE
            ]

    pl.semaphore_wait(barrier, lam_n + pair_n - 2)

    sends = []
    place_copies, index_copies, half_copies, mix_copies = [], [], [], []
    for d in range(1, lam_n):
        peer = lax.rem(lam_me + d, lam_n)
        copy = pltpu.make_async_remote_copy(
            src_ref=place_ref, dst_ref=place_held.at[lam_me],
            send_sem=place_ssem.at[d], recv_sem=place_rsem.at[d],
            device_id={"lam": peer}, device_id_type=MESH,
        )
        copy.start()
        place_copies.append(copy)
    for d in range(1, pair_n):
        peer = lax.rem(pair_me + d, pair_n)
        copy = pltpu.make_async_remote_copy(
            src_ref=index_ref, dst_ref=index_held.at[pair_me],
            send_sem=index_ssem.at[d], recv_sem=index_rsem.at[d],
            device_id={"pair": peer}, device_id_type=MESH,
        )
        copy.start()
        index_copies.append(copy)
    for c in range(chunks):
        row_copies = []
        for d in range(1, lam_n):
            peer = lax.rem(lam_me + d, lam_n)
            copy = pltpu.make_async_remote_copy(
                src_ref=half_send.at[peer, c], dst_ref=half_held.at[c, lam_me],
                send_sem=half_ssem.at[c, d], recv_sem=half_rsem.at[c, d],
                device_id={"lam": peer}, device_id_type=MESH,
            )
            copy.start()
            row_copies.append(copy)
        half_copies.append(row_copies)

    place_held[lam_me] = place_ref[...]
    index_held[pair_me] = index_ref[...]
    for c in range(chunks):
        half_held[c, lam_me] = half_send[lam_me, c]

    for copy in index_copies:
        copy.wait_recv()
    for p in range(pair_n):
        named = index_held[p].astype(jnp.float32)
        low = lax.broadcasted_iota(jnp.int32, (1, LANES), 1) < rows
        line = jnp.where(low, named[0:1], pltpu.roll(named, rows, 1)[1:2])
        column = jnp.transpose(jnp.broadcast_to(line, (LANES, LANES)))
        for b in range(basis // LANES):
            name = (lax.broadcasted_iota(jnp.int32, (LANES, LANES), 1) + b * LANES).astype(jnp.float32)
            hit = one_hot(column == name)
            pick[0, p * rows:(p + 1) * rows, b * LANES:(b + 1) * LANES] = hit[:rows]
            pick[1, p * rows:(p + 1) * rows, b * LANES:(b + 1) * LANES] = hit[rows:]
    occ_rows = lax.dot_general(
        pick[0], occ_ref[...], (((1,), (1,)), ((), ())), preferred_element_type=jnp.float32
    ).astype(jnp.bfloat16)
    lane_i, _ = split_iota((occ_total, occ_total * LANES), 1, LANES)
    widen = one_hot(lax.broadcasted_iota(jnp.int32, lane_i.shape, 0) == lane_i)
    occ_wide_ref[...] = jnp.dot(occ_rows, widen, preferred_element_type=jnp.float32).astype(jnp.bfloat16)
    vir_copy.wait()
    step = 2 * LANES
    for n in range(0, vir_buf.shape[1], step):
        vir_rows_ref[:, n:n + step] = jnp.dot(
            pick[1], vir_buf[:, n:n + step], preferred_element_type=jnp.float32
        ).astype(jnp.bfloat16)

    for copy in place_copies:
        copy.wait_recv()
    place = jnp.transpose(place_held[...].reshape(-1, LANES).astype(jnp.float32)).astype(jnp.bfloat16)

    for c in range(chunks):
        for copy in half_copies[c]:
            copy.wait_recv()
        slots = half_held[c].reshape(-1, basis)
        half_low = jnp.dot(place, slots, preferred_element_type=jnp.float32).astype(jnp.bfloat16)
        for n in range(0, vir_buf.shape[1], step):
            mixed = jnp.dot(half_low, vir_buf[:, n:n + step], preferred_element_type=jnp.float32)
            mixed_t[n:n + step, :] = jnp.transpose(mixed)
        for p in range(pair_n):
            block = mixed_t[p * share:(p + 1) * share, :]
            if share_pad > share:
                block = jnp.concatenate([block, jnp.zeros((share_pad - share, LANES), jnp.float32)], axis=0)
            mix_send[c, p] = block.astype(jnp.bfloat16)
        row_copies = []
        for d in range(1, pair_n):
            peer = lax.rem(pair_me + d, pair_n)
            copy = pltpu.make_async_remote_copy(
                src_ref=mix_send.at[c, peer], dst_ref=mix_held.at[c, pair_me],
                send_sem=mix_ssem.at[c, d], recv_sem=mix_rsem.at[c, d],
                device_id={"pair": peer}, device_id_type=MESH,
            )
            copy.start()
            row_copies.append(copy)
        mix_copies.append(row_copies)
        mix_held[c, pair_me] = mix_send[c, pair_me]

    low_lanes = lax.broadcasted_iota(jnp.int32, (share_pad, LANES), 1) < rows
    for c in range(chunks):
        for copy in mix_copies[c]:
            copy.wait_recv()
        for pp in range(pair_n // 2):
            even = mix_held[c, 2 * pp].astype(jnp.float32)
            odd = mix_held[c, 2 * pp + 1].astype(jnp.float32)
            first = jnp.where(low_lanes, even, pltpu.roll(odd, rows, 1))
            second = jnp.where(low_lanes, pltpu.roll(even, rows, 1), odd)
            lhs_ref[2 * c, :, pp * LANES:(pp + 1) * LANES] = first.astype(jnp.bfloat16)
            lhs_ref[2 * c + 1, :, pp * LANES:(pp + 1) * LANES] = second.astype(jnp.bfloat16)

    for copy in place_copies + index_copies + sum(half_copies, []) + sum(mix_copies, []):
        copy.wait_send()


def product_kernel(share, lhs_ref, occ_wide_ref, vir_rows_ref, out_ref):
    items, share_pad, total_rows = lhs_ref.shape
    occ_wide = jnp.concatenate([occ_wide_ref[...]] * 2, axis=1)
    lhs = lhs_ref[...].reshape(items * share_pad, total_rows)
    step = 2 * LANES
    for n in range(0, vir_rows_ref.shape[1], step):
        weights = occ_wide * vir_rows_ref[:, n:n + step]
        block = jnp.dot(lhs, weights, preferred_element_type=jnp.float32)
        for j in range(items):
            out_ref[j, :, n:n + step] = block[j * share_pad:j * share_pad + share]


def on_device(
    integrals, tile_pair, tile_lam, tile_count, mu_index, nu_index, occupied_coef, virtual_coef
):
    lam_n = lax.axis_size("lam")
    pair_n = lax.axis_size("pair")
    basis, occ_total = occupied_coef.shape
    vir_total = virtual_coef.shape[1]
    rows = mu_index.shape[0]
    slots, prows, blk = integrals.shape[1:4]
    bf16 = jnp.bfloat16
    both = LANES // rows
    occ_share = occ_total // lam_n
    chunks = occ_share // both
    share = vir_total // pair_n
    share_pad = round_up(share, ROW_TILE)
    duo = ROW_TILE // (both * prows)
    groups = slots // duo
    total_rows = rows * pair_n

    vmem = pl.BlockSpec(memory_space=pltpu.VMEM)
    smem = pl.BlockSpec(memory_space=pltpu.SMEM)
    hbm = pl.BlockSpec(memory_space=pl.ANY)
    dma = pltpu.SemaphoreType.DMA
    chunk_rows = slots * both * prows
    lhs, occ_wide, vir_rows = pl.pallas_call(
        functools.partial(exchange_kernel, lam_n, pair_n, chunks, share, share_pad, rows, prows, blk),
        out_shape=(
            jax.ShapeDtypeStruct((occ_share, share_pad, total_rows), bf16),
            jax.ShapeDtypeStruct((total_rows, occ_total * LANES), bf16),
            jax.ShapeDtypeStruct((total_rows, vir_total), bf16),
        ),
        in_specs=[hbm, smem, smem, smem, vmem, vmem, vmem, hbm],
        out_specs=(vmem, vmem, vmem),
        scratch_shapes=[
            pltpu.VMEM((groups, duo * prows * blk, basis), bf16),
            pltpu.VMEM((basis, vir_total), bf16),
            pltpu.VMEM((chunk_rows, LANES), bf16),
            pltpu.VMEM((8, LANES), jnp.int32),
            pltpu.VMEM((lam_n, chunks, chunk_rows, basis), bf16),
            pltpu.VMEM((chunks, lam_n, chunk_rows, basis), bf16),
            pltpu.VMEM((lam_n, chunk_rows, LANES), bf16),
            pltpu.VMEM((pair_n, 8, LANES), jnp.int32),
            pltpu.VMEM((2, total_rows, basis), bf16),
            pltpu.VMEM((vir_total, LANES), jnp.float32),
            pltpu.VMEM((chunks, pair_n, share_pad, LANES), bf16),
            pltpu.VMEM((chunks, pair_n, share_pad, LANES), bf16),
            dma((groups,)),
            dma,
            dma((lam_n,)),
            dma((lam_n,)),
            dma((pair_n,)),
            dma((pair_n,)),
            dma((chunks, lam_n)),
            dma((chunks, lam_n)),
            dma((chunks, pair_n)),
            dma((chunks, pair_n)),
        ],
        compiler_params=pltpu.CompilerParams(
            collective_id=0, has_side_effects=True, vmem_limit_bytes=VMEM_BYTES
        ),
        name="exchange",
    )(
        integrals.reshape(slots * prows * blk, basis), tile_pair, tile_lam, tile_count,
        mu_index[None, :], nu_index[None, :], occupied_coef.T, virtual_coef,
    )

    return pl.pallas_call(
        functools.partial(product_kernel, share),
        out_shape=jax.ShapeDtypeStruct((occ_share, share, occ_total * vir_total), jnp.float32),
        grid=(occ_total,),
        in_specs=[
            pl.BlockSpec((occ_share, share_pad, total_rows), lambda i: (0, 0, 0)),
            pl.BlockSpec((total_rows, LANES), lambda i: (0, i)),
            pl.BlockSpec((total_rows, vir_total), lambda i: (0, 0)),
        ],
        out_specs=pl.BlockSpec((occ_share, share, vir_total), lambda i: (0, 0, i)),
        compiler_params=pltpu.CompilerParams(vmem_limit_bytes=VMEM_BYTES),
        name="product",
    )(lhs, occ_wide, vir_rows)


def solution(mesh):
    placed = (
        P("pair", "lam", None, None, None),
        P("pair", "lam"),
        P("pair", "lam"),
        P("pair", "lam"),
        P("pair"),
        P("pair"),
        P(),
        P(),
    )
    return jax.shard_map(
        on_device, mesh=mesh, in_specs=placed, out_specs=P("lam", "pair", None), check_vma=False
    )
```

```python
import functools

import jax
import jax.numpy as jnp
from jax import lax
from jax.experimental import pallas as pl
from jax.experimental.pallas import tpu as pltpu
from jax.sharding import PartitionSpec as P

LANES = 128
ROW_TILE = 16
VMEM_BYTES = 64 * 1024 * 1024
MESH = pl.DeviceIdType.MESH


def round_up(value, step):
    return (value + step - 1) // step * step


def bits_of(size):
    return size.bit_length() - 1


def split_iota(shape, dim, *sizes):
    left = lax.broadcasted_iota(jnp.int32, shape, dim)
    parts = []
    for size in reversed(sizes):
        parts.append(left & (size - 1))
        left = left >> bits_of(size)
    return [left] + parts[::-1]


def one_hot(hit):
    return jnp.where(hit, 1.0, 0.0).astype(jnp.bfloat16)


def exchange_kernel(
    lam_n, pair_n, chunks, share, share_pad, rows, prows, blk,
    tiles_ref, pair_hbm, lam_hbm, count_hbm, mu_hbm, nu_hbm, occ_hbm, vir_ref,
    lhs_out, occ_wide_out, vir_rows_out,
    lhs_ref, occ_wide_ref, vir_rows_ref, out_sem,
    pair_ref, lam_ref, count_ref, mu_ref, nu_ref, occ_ref, small_sem,
    tile_buf, vir_buf, place_ref, index_ref, half_send, half_held, place_held, index_held, pick, mixed_t,
    mix_send, mix_held,
    tile_sem, vir_sem, place_ssem, place_rsem, index_ssem, index_rsem,
    half_ssem, half_rsem, mix_ssem, mix_rsem,
):
    lam_me = lax.axis_index("lam")
    pair_me = lax.axis_index("pair")
    groups = tile_buf.shape[0]
    depth = tile_buf.shape[1]
    basis = vir_buf.shape[0]
    occ_total = occ_ref.shape[0]
    both = LANES // rows
    slots = pair_ref.shape[1]
    duo = slots // groups

    barrier = pltpu.get_barrier_semaphore()
    for d in range(1, lam_n):
        pl.semaphore_signal(barrier, inc=1, device_id={"lam": lax.rem(lam_me + d, lam_n)}, device_id_type=MESH)
    for d in range(1, pair_n):
        pl.semaphore_signal(barrier, inc=1, device_id={"pair": lax.rem(pair_me + d, pair_n)}, device_id_type=MESH)

    small_copies = [
        pltpu.make_async_copy(source, target, small_sem.at[n])
        for n, (source, target) in enumerate([
            (pair_hbm, pair_ref), (lam_hbm, lam_ref), (count_hbm, count_ref),
            (mu_hbm, mu_ref), (nu_hbm, nu_ref), (occ_hbm, occ_ref),
        ])
    ]
    for copy in small_copies:
        copy.start()
    tile_copies = [
        pltpu.make_async_copy(tiles_ref.at[pl.ds(q * depth, depth)], tile_buf.at[q], tile_sem.at[q])
        for q in range(groups)
    ]
    vir_copy = pltpu.make_async_copy(vir_ref, vir_buf, vir_sem)
    for copy in tile_copies:
        copy.start()
    vir_copy.start()

    for copy in small_copies:
        copy.wait()

    slot, row_j, row_k = split_iota((slots * both * prows, LANES), 0, both, prows)
    lane_j, lane_r = split_iota((slots * both * prows, LANES), 1, rows)
    goal = jnp.zeros_like(slot)
    for t in range(slots):
        goal = jnp.where(slot == t, pair_ref[0, t], goal)
    place_ref[...] = one_hot((row_j == lane_j) & (lane_r == goal * prows + row_k))
    index_ref[...] = jnp.zeros_like(index_ref)
    index_ref[0:1, 0:rows] = mu_ref[...]
    index_ref[1:2, 0:rows] = nu_ref[...]

    lam_rows = basis // lam_n
    width = slots * prows * blk
    lane_t, _, lane_m = split_iota((1, width), 1, prows, blk)
    source = jnp.zeros_like(lane_t)
    for t in range(slots):
        first = jnp.where(count_ref[0, 0] > t, lam_ref[0, t] * blk - lam_me * lam_rows, -2 * basis)
        source = jnp.where(lane_t == t, first, source)
    source = source + lane_m
    chosen = one_hot(lax.broadcasted_iota(jnp.int32, (lam_rows, width), 0) == source)
    occ_own = occ_ref[:, pl.ds(pl.multiple_of(lam_me * lam_rows, lam_rows), lam_rows)]
    occ_tiles = jnp.dot(occ_own, chosen, preferred_element_type=jnp.float32).astype(jnp.bfloat16)
    height = lam_n * chunks * ROW_TILE
    group, _, repeat_j, _ = split_iota((height, occ_total), 0, duo, both, prows)
    repeat = one_hot(lax.broadcasted_iota(jnp.int32, (height, occ_total), 1) == group * both + repeat_j)
    factor = jnp.dot(repeat, occ_tiles, preferred_element_type=jnp.float32)
    _, row_t, _, row_k = split_iota((height, width), 0, duo, both, prows)
    lane_t, lane_k, _ = split_iota((height, width), 1, prows, blk)
    spread = jnp.where((row_t == (lane_t & (duo - 1))) & (row_k == lane_k), factor, 0.0).astype(jnp.bfloat16)

    for q in range(groups):
        tile_copies[q].wait()
        part = jnp.dot(
            spread[:, q * depth:(q + 1) * depth], tile_buf[q], preferred_element_type=jnp.float32
        ).astype(jnp.bfloat16)
        for g in range(lam_n * chunks):
            half_send[g // chunks, g % chunks, q * ROW_TILE:(q + 1) * ROW_TILE, :] = part[
                g * ROW_TILE:(g + 1) * ROW_TILE
            ]

    pl.semaphore_wait(barrier, lam_n + pair_n - 2)

    sends = []
    place_copies, index_copies, half_copies, mix_copies = [], [], [], []
    for d in range(1, lam_n):
        peer = lax.rem(lam_me + d, lam_n)
        copy = pltpu.make_async_remote_copy(
            src_ref=place_ref, dst_ref=place_held.at[lam_me],
            send_sem=place_ssem.at[d], recv_sem=place_rsem.at[d],
            device_id={"lam": peer}, device_id_type=MESH,
        )
        copy.start()
        place_copies.append(copy)
    for d in range(1, pair_n):
        peer = lax.rem(pair_me + d, pair_n)
        copy = pltpu.make_async_remote_copy(
            src_ref=index_ref, dst_ref=index_held.at[pair_me],
            send_sem=index_ssem.at[d], recv_sem=index_rsem.at[d],
            device_id={"pair": peer}, device_id_type=MESH,
        )
        copy.start()
        index_copies.append(copy)
    for c in range(chunks):
        row_copies = []
        for d in range(1, lam_n):
            peer = lax.rem(lam_me + d, lam_n)
            copy = pltpu.make_async_remote_copy(
                src_ref=half_send.at[peer, c], dst_ref=half_held.at[c, lam_me],
                send_sem=half_ssem.at[c, d], recv_sem=half_rsem.at[c, d],
                device_id={"lam": peer}, device_id_type=MESH,
            )
            copy.start()
            row_copies.append(copy)
        half_copies.append(row_copies)

    place_held[lam_me] = place_ref[...]
    index_held[pair_me] = index_ref[...]
    for c in range(chunks):
        half_held[c, lam_me] = half_send[lam_me, c]

    for copy in index_copies:
        copy.wait_recv()
    for p in range(pair_n):
        named = index_held[p].astype(jnp.float32)
        low = lax.broadcasted_iota(jnp.int32, (1, LANES), 1) < rows
        line = jnp.where(low, named[0:1], pltpu.roll(named, rows, 1)[1:2])
        column = jnp.transpose(jnp.broadcast_to(line, (LANES, LANES)))
        for b in range(basis // LANES):
            name = (lax.broadcasted_iota(jnp.int32, (LANES, LANES), 1) + b * LANES).astype(jnp.float32)
            hit = one_hot(column == name)
            pick[0, p * rows:(p + 1) * rows, b * LANES:(b + 1) * LANES] = hit[:rows]
            pick[1, p * rows:(p + 1) * rows, b * LANES:(b + 1) * LANES] = hit[rows:]
    occ_rows = lax.dot_general(
        pick[0], occ_ref[...], (((1,), (1,)), ((), ())), preferred_element_type=jnp.float32
    ).astype(jnp.bfloat16)
    lane_i, _ = split_iota((occ_total, occ_total * LANES), 1, LANES)
    widen = one_hot(lax.broadcasted_iota(jnp.int32, lane_i.shape, 0) == lane_i)
    occ_wide_ref[...] = jnp.dot(occ_rows, widen, preferred_element_type=jnp.float32).astype(jnp.bfloat16)
    vir_copy.wait()
    step = 2 * LANES
    for n in range(0, vir_buf.shape[1], step):
        vir_rows_ref[:, n:n + step] = jnp.dot(
            pick[1], vir_buf[:, n:n + step], preferred_element_type=jnp.float32
        ).astype(jnp.bfloat16)

    out_copies = [
        pltpu.make_async_copy(occ_wide_ref, occ_wide_out, out_sem.at[0]),
        pltpu.make_async_copy(vir_rows_ref, vir_rows_out, out_sem.at[1]),
    ]
    for copy in out_copies:
        copy.start()

    for copy in place_copies:
        copy.wait_recv()
    place = jnp.transpose(place_held[...].reshape(-1, LANES).astype(jnp.float32)).astype(jnp.bfloat16)

    for c in range(chunks):
        for copy in half_copies[c]:
            copy.wait_recv()
        slots = half_held[c].reshape(-1, basis)
        half_low = jnp.dot(place, slots, preferred_element_type=jnp.float32).astype(jnp.bfloat16)
        for n in range(0, vir_buf.shape[1], step):
            mixed = jnp.dot(half_low, vir_buf[:, n:n + step], preferred_element_type=jnp.float32)
            mixed_t[n:n + step, :] = jnp.transpose(mixed)
        for p in range(pair_n):
            block = mixed_t[p * share:(p + 1) * share, :]
            if share_pad > share:
                block = jnp.concatenate([block, jnp.zeros((share_pad - share, LANES), jnp.float32)], axis=0)
            mix_send[c, p] = block.astype(jnp.bfloat16)
        row_copies = []
        for d in range(1, pair_n):
            peer = lax.rem(pair_me + d, pair_n)
            copy = pltpu.make_async_remote_copy(
                src_ref=mix_send.at[c, peer], dst_ref=mix_held.at[c, pair_me],
                send_sem=mix_ssem.at[c, d], recv_sem=mix_rsem.at[c, d],
                device_id={"pair": peer}, device_id_type=MESH,
            )
            copy.start()
            row_copies.append(copy)
        mix_copies.append(row_copies)
        mix_held[c, pair_me] = mix_send[c, pair_me]

    low_lanes = lax.broadcasted_iota(jnp.int32, (share_pad, LANES), 1) < rows
    for c in range(chunks):
        for copy in mix_copies[c]:
            copy.wait_recv()
        for pp in range(pair_n // 2):
            even = mix_held[c, 2 * pp].astype(jnp.float32)
            odd = mix_held[c, 2 * pp + 1].astype(jnp.float32)
            first = jnp.where(low_lanes, even, pltpu.roll(odd, rows, 1))
            second = jnp.where(low_lanes, pltpu.roll(even, rows, 1), odd)
            lhs_ref[2 * c, :, pp * LANES:(pp + 1) * LANES] = first.astype(jnp.bfloat16)
            lhs_ref[2 * c + 1, :, pp * LANES:(pp + 1) * LANES] = second.astype(jnp.bfloat16)
        copy = pltpu.make_async_copy(
            lhs_ref.at[pl.ds(2 * c, 2)], lhs_out.at[pl.ds(2 * c, 2)], out_sem.at[2 + c]
        )
        copy.start()
        out_copies.append(copy)

    for copy in place_copies + index_copies + sum(half_copies, []) + sum(mix_copies, []):
        copy.wait_send()
    for copy in out_copies:
        copy.wait()


def product_kernel(share, lhs_ref, occ_wide_ref, vir_rows_ref, out_ref, held, sems):
    items, share_pad, total_rows = lhs_ref.shape
    vir_total = vir_rows_ref.shape[1]
    step_i = pl.program_id(0)
    last = pl.num_programs(0) - 1
    step = 2 * LANES
    middle = round_up(vir_total // 2, step)
    parts = ((0, middle), (middle, vir_total))

    def copies(at, part):
        begin, end = parts[part]
        slot = lax.rem(at, 2)
        columns = pl.ds(pl.multiple_of(at * vir_total + begin, LANES), end - begin)
        return [
            pltpu.make_async_copy(
                held.at[slot, j, :, pl.ds(begin, end - begin)], out_ref.at[j, :, columns], sems.at[slot, part, j]
            )
            for j in range(items)
        ]

    @pl.when(step_i >= 2)
    def _():
        for part in range(2):
            for copy in copies(step_i - 2, part):
                copy.wait()

    slot_now = lax.rem(step_i, 2)
    occ_wide = jnp.concatenate([occ_wide_ref[...]] * 2, axis=1)
    lhs = lhs_ref[...].reshape(items * share_pad, total_rows)
    for part in range(2):
        for n in range(*parts[part], step):
            weights = occ_wide * vir_rows_ref[:, n:n + step]
            block = jnp.dot(lhs, weights, preferred_element_type=jnp.float32)
            held[slot_now, :, :, n:n + step] = block.reshape(items, share_pad, step)[:, :share]
        for copy in copies(step_i, part):
            copy.start()

    @pl.when(step_i == last)
    def _():
        for at in (last - 1, last):
            for part in range(2):
                for copy in copies(at, part):
                    copy.wait()


def on_device(
    integrals, tile_pair, tile_lam, tile_count, mu_index, nu_index, occupied_coef, virtual_coef
):
    lam_n = lax.axis_size("lam")
    pair_n = lax.axis_size("pair")
    basis, occ_total = occupied_coef.shape
    vir_total = virtual_coef.shape[1]
    rows = mu_index.shape[0]
    slots, prows, blk = integrals.shape[1:4]
    bf16 = jnp.bfloat16
    both = LANES // rows
    occ_share = occ_total // lam_n
    chunks = occ_share // both
    share = vir_total // pair_n
    share_pad = round_up(share, ROW_TILE)
    duo = ROW_TILE // (both * prows)
    groups = slots // duo
    total_rows = rows * pair_n

    pinned = pl.BlockSpec(memory_space=pltpu.HBM)
    dma = pltpu.SemaphoreType.DMA
    chunk_rows = slots * both * prows
    lhs, occ_wide, vir_rows = pl.pallas_call(
        functools.partial(exchange_kernel, lam_n, pair_n, chunks, share, share_pad, rows, prows, blk),
        out_shape=(
            jax.ShapeDtypeStruct((occ_share, share_pad, total_rows), bf16),
            jax.ShapeDtypeStruct((total_rows, occ_total * LANES), bf16),
            jax.ShapeDtypeStruct((total_rows, vir_total), bf16),
        ),
        in_specs=[pinned] * 8,
        out_specs=(pinned, pinned, pinned),
        scratch_shapes=[
            pltpu.VMEM((occ_share, share_pad, total_rows), bf16),
            pltpu.VMEM((total_rows, occ_total * LANES), bf16),
            pltpu.VMEM((total_rows, vir_total), bf16),
            dma((2 + chunks,)),
            pltpu.SMEM((1, slots), jnp.int32),
            pltpu.SMEM((1, slots), jnp.int32),
            pltpu.SMEM((1, 1), jnp.int32),
            pltpu.VMEM((1, rows), jnp.int32),
            pltpu.VMEM((1, rows), jnp.int32),
            pltpu.VMEM((occ_total, basis), bf16),
            dma((6,)),
            pltpu.VMEM((groups, duo * prows * blk, basis), bf16),
            pltpu.VMEM((basis, vir_total), bf16),
            pltpu.VMEM((chunk_rows, LANES), bf16),
            pltpu.VMEM((8, LANES), jnp.int32),
            pltpu.VMEM((lam_n, chunks, chunk_rows, basis), bf16),
            pltpu.VMEM((chunks, lam_n, chunk_rows, basis), bf16),
            pltpu.VMEM((lam_n, chunk_rows, LANES), bf16),
            pltpu.VMEM((pair_n, 8, LANES), jnp.int32),
            pltpu.VMEM((2, total_rows, basis), bf16),
            pltpu.VMEM((vir_total, LANES), jnp.float32),
            pltpu.VMEM((chunks, pair_n, share_pad, LANES), bf16),
            pltpu.VMEM((chunks, pair_n, share_pad, LANES), bf16),
            dma((groups,)),
            dma,
            dma((lam_n,)),
            dma((lam_n,)),
            dma((pair_n,)),
            dma((pair_n,)),
            dma((chunks, lam_n)),
            dma((chunks, lam_n)),
            dma((chunks, pair_n)),
            dma((chunks, pair_n)),
        ],
        compiler_params=pltpu.CompilerParams(
            collective_id=0, has_side_effects=True, vmem_limit_bytes=VMEM_BYTES
        ),
        name="exchange",
    )(
        integrals.reshape(slots * prows * blk, basis), tile_pair, tile_lam, tile_count,
        mu_index[None, :], nu_index[None, :], occupied_coef.T, virtual_coef,
    )

    return pl.pallas_call(
        functools.partial(product_kernel, share),
        out_shape=jax.ShapeDtypeStruct((occ_share, share, occ_total * vir_total), jnp.float32),
        grid=(occ_total,),
        in_specs=[
            pl.BlockSpec((occ_share, share_pad, total_rows), lambda i: (0, 0, 0)),
            pl.BlockSpec((total_rows, LANES), lambda i: (0, i)),
            pl.BlockSpec((total_rows, vir_total), lambda i: (0, 0)),
        ],
        out_specs=pl.BlockSpec(memory_space=pl.ANY),
        scratch_shapes=[
            pltpu.VMEM((2, occ_share, share, vir_total), jnp.float32),
            dma((2, 2, occ_share)),
        ],
        compiler_params=pltpu.CompilerParams(vmem_limit_bytes=VMEM_BYTES),
        name="product",
    )(lhs, occ_wide, vir_rows)


def solution(mesh):
    placed = (
        P("pair", "lam", None, None, None),
        P("pair", "lam"),
        P("pair", "lam"),
        P("pair", "lam"),
        P("pair"),
        P("pair"),
        P(),
        P(),
    )
    return jax.shard_map(
        on_device, mesh=mesh, in_specs=placed, out_specs=P("lam", "pair", None), check_vma=False
    )
```

```python
import functools

import jax
import jax.numpy as jnp
from jax import lax
from jax.experimental import pallas as pl
from jax.experimental.pallas import tpu as pltpu
from jax.sharding import PartitionSpec as P

LANES = 128
ROW_TILE = 16
VMEM_BYTES = 64 * 1024 * 1024
MESH = pl.DeviceIdType.MESH


def round_up(value, step):
    return (value + step - 1) // step * step


def bits_of(size):
    return size.bit_length() - 1


def split_iota(shape, dim, *sizes):
    left = lax.broadcasted_iota(jnp.int32, shape, dim)
    parts = []
    for size in reversed(sizes):
        parts.append(left & (size - 1))
        left = left >> bits_of(size)
    return [left] + parts[::-1]


def one_hot(hit):
    return jnp.where(hit, 1.0, 0.0).astype(jnp.bfloat16)


def exchange_kernel(
    lam_n, pair_n, chunks, share, share_pad, rows, prows, blk,
    tiles_ref, pair_hbm, lam_hbm, count_hbm, mu_hbm, nu_hbm, occ_hbm, vir_ref,
    lhs_out, occ_wide_out, vir_rows_out,
    lhs_ref, occ_wide_ref, vir_rows_ref, out_sem,
    pair_ref, lam_ref, count_ref, mu_ref, nu_ref, occ_ref, small_sem,
    tile_buf, vir_buf, place_ref, index_ref, half_send, half_held, place_held, index_held, pick, mixed_t,
    mix_send, mix_held,
    tile_sem, vir_sem, place_ssem, place_rsem, index_ssem, index_rsem,
    half_ssem, half_rsem, mix_ssem, mix_rsem,
):
    lam_me = lax.axis_index("lam")
    pair_me = lax.axis_index("pair")
    groups = tile_buf.shape[0]
    depth = tile_buf.shape[1]
    basis = vir_buf.shape[0]
    occ_total = occ_ref.shape[0]
    both = LANES // rows
    slots = pair_ref.shape[1]
    duo = slots // groups

    barrier = pltpu.get_barrier_semaphore()
    for d in range(1, lam_n):
        pl.semaphore_signal(barrier, inc=1, device_id={"lam": lax.rem(lam_me + d, lam_n)}, device_id_type=MESH)
    for d in range(1, pair_n):
        pl.semaphore_signal(barrier, inc=1, device_id={"pair": lax.rem(pair_me + d, pair_n)}, device_id_type=MESH)

    small_copies = [
        pltpu.make_async_copy(source, target, small_sem.at[n])
        for n, (source, target) in enumerate([
            (pair_hbm, pair_ref), (lam_hbm, lam_ref), (count_hbm, count_ref),
            (mu_hbm, mu_ref), (nu_hbm, nu_ref), (occ_hbm, occ_ref),
        ])
    ]
    for copy in small_copies:
        copy.start()
    tile_copies = [
        pltpu.make_async_copy(tiles_ref.at[pl.ds(q * depth, depth)], tile_buf.at[q], tile_sem.at[q])
        for q in range(groups)
    ]
    vir_copy = pltpu.make_async_copy(vir_ref, vir_buf, vir_sem)
    for copy in tile_copies:
        copy.start()
    vir_copy.start()

    for copy in small_copies:
        copy.wait()

    slot, row_j, row_k = split_iota((slots * both * prows, LANES), 0, both, prows)
    lane_j, lane_r = split_iota((slots * both * prows, LANES), 1, rows)
    goal = jnp.zeros_like(slot)
    for t in range(slots):
        goal = jnp.where(slot == t, pair_ref[0, t], goal)
    place_ref[...] = one_hot((row_j == lane_j) & (lane_r == goal * prows + row_k))
    index_ref[...] = jnp.zeros_like(index_ref)
    index_ref[0:1, 0:rows] = mu_ref[...]
    index_ref[1:2, 0:rows] = nu_ref[...]

    lam_rows = basis // lam_n
    width = slots * prows * blk
    lane_t, _, lane_m = split_iota((1, width), 1, prows, blk)
    source = jnp.zeros_like(lane_t)
    for t in range(slots):
        first = jnp.where(count_ref[0, 0] > t, lam_ref[0, t] * blk - lam_me * lam_rows, -2 * basis)
        source = jnp.where(lane_t == t, first, source)
    source = source + lane_m
    chosen = one_hot(lax.broadcasted_iota(jnp.int32, (lam_rows, width), 0) == source)
    occ_own = occ_ref[:, pl.ds(pl.multiple_of(lam_me * lam_rows, lam_rows), lam_rows)]
    occ_tiles = jnp.dot(occ_own, chosen, preferred_element_type=jnp.float32).astype(jnp.bfloat16)
    height = lam_n * chunks * ROW_TILE
    group, _, repeat_j, _ = split_iota((height, occ_total), 0, duo, both, prows)
    repeat = one_hot(lax.broadcasted_iota(jnp.int32, (height, occ_total), 1) == group * both + repeat_j)
    factor = jnp.dot(repeat, occ_tiles, preferred_element_type=jnp.float32)
    _, row_t, _, row_k = split_iota((height, width), 0, duo, both, prows)
    lane_t, lane_k, _ = split_iota((height, width), 1, prows, blk)
    spread = jnp.where((row_t == (lane_t & (duo - 1))) & (row_k == lane_k), factor, 0.0).astype(jnp.bfloat16)

    for q in range(groups):
        tile_copies[q].wait()
        part = jnp.dot(
            spread[:, q * depth:(q + 1) * depth], tile_buf[q], preferred_element_type=jnp.float32
        ).astype(jnp.bfloat16)
        for g in range(lam_n * chunks):
            half_send[g // chunks, g % chunks, q * ROW_TILE:(q + 1) * ROW_TILE, :] = part[
                g * ROW_TILE:(g + 1) * ROW_TILE
            ]

    pl.semaphore_wait(barrier, lam_n + pair_n - 2)

    place_copies, index_copies, half_copies, mix_copies = [], [], [], []
    for d in range(1, lam_n):
        peer = lax.rem(lam_me + d, lam_n)
        copy = pltpu.make_async_remote_copy(
            src_ref=place_ref, dst_ref=place_held.at[lam_me],
            send_sem=place_ssem.at[d], recv_sem=place_rsem.at[d],
            device_id={"lam": peer}, device_id_type=MESH,
        )
        copy.start()
        place_copies.append(copy)
    for d in range(1, pair_n):
        peer = lax.rem(pair_me + d, pair_n)
        copy = pltpu.make_async_remote_copy(
            src_ref=index_ref, dst_ref=index_held.at[pair_me],
            send_sem=index_ssem.at[d], recv_sem=index_rsem.at[d],
            device_id={"pair": peer}, device_id_type=MESH,
        )
        copy.start()
        index_copies.append(copy)
    def send_half(c):
        row_copies = []
        for d in range(lam_n - 1, 0, -1):
            peer = lax.rem(lam_me + d, lam_n)
            copy = pltpu.make_async_remote_copy(
                src_ref=half_send.at[peer, c], dst_ref=half_held.at[c, lam_me],
                send_sem=half_ssem.at[c, d], recv_sem=half_rsem.at[c, d],
                device_id={"lam": peer}, device_id_type=MESH,
            )
            copy.start()
            row_copies.append(copy)
        half_copies.append(row_copies)

    send_half(0)
    place_held[lam_me] = place_ref[...]
    index_held[pair_me] = index_ref[...]
    for c in range(chunks):
        half_held[c, lam_me] = half_send[lam_me, c]

    for copy in index_copies:
        copy.wait_recv()
    for p in range(pair_n):
        named = index_held[p].astype(jnp.float32)
        low = lax.broadcasted_iota(jnp.int32, (1, LANES), 1) < rows
        line = jnp.where(low, named[0:1], pltpu.roll(named, rows, 1)[1:2])
        column = jnp.transpose(jnp.broadcast_to(line, (LANES, LANES)))
        for b in range(basis // LANES):
            name = (lax.broadcasted_iota(jnp.int32, (LANES, LANES), 1) + b * LANES).astype(jnp.float32)
            hit = one_hot(column == name)
            pick[0, p * rows:(p + 1) * rows, b * LANES:(b + 1) * LANES] = hit[:rows]
            pick[1, p * rows:(p + 1) * rows, b * LANES:(b + 1) * LANES] = hit[rows:]
    occ_rows = lax.dot_general(
        pick[0], occ_ref[...], (((1,), (1,)), ((), ())), preferred_element_type=jnp.float32
    ).astype(jnp.bfloat16)
    lane_i, _ = split_iota((occ_total, occ_total * LANES), 1, LANES)
    widen = one_hot(lax.broadcasted_iota(jnp.int32, lane_i.shape, 0) == lane_i)
    occ_wide_ref[...] = jnp.dot(occ_rows, widen, preferred_element_type=jnp.float32).astype(jnp.bfloat16)
    vir_copy.wait()
    step = 2 * LANES
    for n in range(0, vir_buf.shape[1], step):
        vir_rows_ref[:, n:n + step] = jnp.dot(
            pick[1], vir_buf[:, n:n + step], preferred_element_type=jnp.float32
        ).astype(jnp.bfloat16)

    out_copies = [
        pltpu.make_async_copy(occ_wide_ref, occ_wide_out, out_sem.at[0]),
        pltpu.make_async_copy(vir_rows_ref, vir_rows_out, out_sem.at[1]),
    ]
    for copy in out_copies:
        copy.start()

    for c in range(1, chunks):
        for copy in half_copies[c - 1]:
            copy.wait_send()
        send_half(c)

    for copy in place_copies:
        copy.wait_recv()
    place = jnp.transpose(place_held[...].reshape(-1, LANES).astype(jnp.float32)).astype(jnp.bfloat16)

    for c in range(chunks):
        for copy in half_copies[c]:
            copy.wait_recv()
        slots = half_held[c].reshape(-1, basis)
        half_low = jnp.dot(place, slots, preferred_element_type=jnp.float32).astype(jnp.bfloat16)
        for n in range(0, vir_buf.shape[1], step):
            mixed = jnp.dot(half_low, vir_buf[:, n:n + step], preferred_element_type=jnp.float32)
            mixed_t[n:n + step, :] = jnp.transpose(mixed)
        for p in range(pair_n):
            block = mixed_t[p * share:(p + 1) * share, :]
            if share_pad > share:
                block = jnp.concatenate([block, jnp.zeros((share_pad - share, LANES), jnp.float32)], axis=0)
            mix_send[c, p] = block.astype(jnp.bfloat16)
        row_copies = []
        for d in range(1, pair_n):
            peer = lax.rem(pair_me + d, pair_n)
            copy = pltpu.make_async_remote_copy(
                src_ref=mix_send.at[c, peer], dst_ref=mix_held.at[c, pair_me],
                send_sem=mix_ssem.at[c, d], recv_sem=mix_rsem.at[c, d],
                device_id={"pair": peer}, device_id_type=MESH,
            )
            copy.start()
            row_copies.append(copy)
        mix_copies.append(row_copies)
        mix_held[c, pair_me] = mix_send[c, pair_me]

    low_lanes = lax.broadcasted_iota(jnp.int32, (share_pad, LANES), 1) < rows
    for c in range(chunks):
        for copy in mix_copies[c]:
            copy.wait_recv()
        for pp in range(pair_n // 2):
            even = mix_held[c, 2 * pp].astype(jnp.float32)
            odd = mix_held[c, 2 * pp + 1].astype(jnp.float32)
            first = jnp.where(low_lanes, even, pltpu.roll(odd, rows, 1))
            second = jnp.where(low_lanes, pltpu.roll(even, rows, 1), odd)
            lhs_ref[2 * c, :, pp * LANES:(pp + 1) * LANES] = first.astype(jnp.bfloat16)
            lhs_ref[2 * c + 1, :, pp * LANES:(pp + 1) * LANES] = second.astype(jnp.bfloat16)
        copy = pltpu.make_async_copy(
            lhs_ref.at[pl.ds(2 * c, 2)], lhs_out.at[pl.ds(2 * c, 2)], out_sem.at[2 + c]
        )
        copy.start()
        out_copies.append(copy)

    for copy in place_copies + index_copies + half_copies[-1] + sum(mix_copies, []):
        copy.wait_send()
    for copy in out_copies:
        copy.wait()


def product_kernel(share, lhs_ref, occ_wide_ref, vir_rows_ref, out_ref, held, sems):
    items, share_pad, total_rows = lhs_ref.shape
    vir_total = vir_rows_ref.shape[1]
    step_i = pl.program_id(0)
    last = pl.num_programs(0) - 1
    step = 2 * LANES
    middle = round_up(vir_total // 2, step)
    parts = ((0, middle), (middle, vir_total))

    def copies(at, part):
        begin, end = parts[part]
        slot = lax.rem(at, 2)
        columns = pl.ds(pl.multiple_of(at * vir_total + begin, LANES), end - begin)
        return [
            pltpu.make_async_copy(
                held.at[slot, j, :, pl.ds(begin, end - begin)], out_ref.at[j, :, columns], sems.at[slot, part, j]
            )
            for j in range(items)
        ]

    @pl.when(step_i >= 2)
    def _():
        for part in range(2):
            for copy in copies(step_i - 2, part):
                copy.wait()

    slot_now = lax.rem(step_i, 2)
    lhs = lhs_ref[...].reshape(items * share_pad, total_rows)
    for part in range(2):
        begin, end = parts[part]
        occ_wide = jnp.concatenate([occ_wide_ref[...]] * ((end - begin) // LANES), axis=1)
        weights = occ_wide * vir_rows_ref[:, begin:end]
        block = jnp.dot(lhs, weights, preferred_element_type=jnp.float32)
        held[slot_now, :, :, begin:end] = block.reshape(items, share_pad, end - begin)[:, :share]
        for copy in copies(step_i, part):
            copy.start()

    @pl.when(step_i == last)
    def _():
        for at in (last - 1, last):
            for part in range(2):
                for copy in copies(at, part):
                    copy.wait()


def on_device(
    integrals, tile_pair, tile_lam, tile_count, mu_index, nu_index, occupied_coef, virtual_coef
):
    lam_n = lax.axis_size("lam")
    pair_n = lax.axis_size("pair")
    basis, occ_total = occupied_coef.shape
    vir_total = virtual_coef.shape[1]
    rows = mu_index.shape[0]
    slots, prows, blk = integrals.shape[1:4]
    bf16 = jnp.bfloat16
    both = LANES // rows
    occ_share = occ_total // lam_n
    chunks = occ_share // both
    share = vir_total // pair_n
    share_pad = round_up(share, ROW_TILE)
    duo = ROW_TILE // (both * prows)
    groups = slots // duo
    total_rows = rows * pair_n

    pinned = pl.BlockSpec(memory_space=pltpu.HBM)
    dma = pltpu.SemaphoreType.DMA
    chunk_rows = slots * both * prows
    lhs, occ_wide, vir_rows = pl.pallas_call(
        functools.partial(exchange_kernel, lam_n, pair_n, chunks, share, share_pad, rows, prows, blk),
        out_shape=(
            jax.ShapeDtypeStruct((occ_share, share_pad, total_rows), bf16),
            jax.ShapeDtypeStruct((total_rows, occ_total * LANES), bf16),
            jax.ShapeDtypeStruct((total_rows, vir_total), bf16),
        ),
        in_specs=[pinned] * 8,
        out_specs=(pinned, pinned, pinned),
        scratch_shapes=[
            pltpu.VMEM((occ_share, share_pad, total_rows), bf16),
            pltpu.VMEM((total_rows, occ_total * LANES), bf16),
            pltpu.VMEM((total_rows, vir_total), bf16),
            dma((2 + chunks,)),
            pltpu.SMEM((1, slots), jnp.int32),
            pltpu.SMEM((1, slots), jnp.int32),
            pltpu.SMEM((1, 1), jnp.int32),
            pltpu.VMEM((1, rows), jnp.int32),
            pltpu.VMEM((1, rows), jnp.int32),
            pltpu.VMEM((occ_total, basis), bf16),
            dma((6,)),
            pltpu.VMEM((groups, duo * prows * blk, basis), bf16),
            pltpu.VMEM((basis, vir_total), bf16),
            pltpu.VMEM((chunk_rows, LANES), bf16),
            pltpu.VMEM((8, LANES), jnp.int32),
            pltpu.VMEM((lam_n, chunks, chunk_rows, basis), bf16),
            pltpu.VMEM((chunks, lam_n, chunk_rows, basis), bf16),
            pltpu.VMEM((lam_n, chunk_rows, LANES), bf16),
            pltpu.VMEM((pair_n, 8, LANES), jnp.int32),
            pltpu.VMEM((2, total_rows, basis), bf16),
            pltpu.VMEM((vir_total, LANES), jnp.float32),
            pltpu.VMEM((chunks, pair_n, share_pad, LANES), bf16),
            pltpu.VMEM((chunks, pair_n, share_pad, LANES), bf16),
            dma((groups,)),
            dma,
            dma((lam_n,)),
            dma((lam_n,)),
            dma((pair_n,)),
            dma((pair_n,)),
            dma((chunks, lam_n)),
            dma((chunks, lam_n)),
            dma((chunks, pair_n)),
            dma((chunks, pair_n)),
        ],
        compiler_params=pltpu.CompilerParams(
            collective_id=0, has_side_effects=True, vmem_limit_bytes=VMEM_BYTES
        ),
        name="exchange",
    )(
        integrals.reshape(slots * prows * blk, basis), tile_pair, tile_lam, tile_count,
        mu_index[None, :], nu_index[None, :], occupied_coef.T, virtual_coef,
    )

    return pl.pallas_call(
        functools.partial(product_kernel, share),
        out_shape=jax.ShapeDtypeStruct((occ_share, share, occ_total * vir_total), jnp.float32),
        grid=(occ_total,),
        in_specs=[
            pl.BlockSpec((occ_share, share_pad, total_rows), lambda i: (0, 0, 0)),
            pl.BlockSpec((total_rows, LANES), lambda i: (0, i)),
            pl.BlockSpec((total_rows, vir_total), lambda i: (0, 0)),
        ],
        out_specs=pl.BlockSpec(memory_space=pl.ANY),
        scratch_shapes=[
            pltpu.VMEM((2, occ_share, share, vir_total), jnp.float32),
            dma((2, 2, occ_share)),
        ],
        compiler_params=pltpu.CompilerParams(vmem_limit_bytes=VMEM_BYTES),
        name="product",
    )(lhs, occ_wide, vir_rows)


def solution(mesh):
    placed = (
        P("pair", "lam", None, None, None),
        P("pair", "lam"),
        P("pair", "lam"),
        P("pair", "lam"),
        P("pair"),
        P("pair"),
        P(),
        P(),
    )
    return jax.shard_map(
        on_device, mesh=mesh, in_specs=placed, out_specs=P("lam", "pair", None), check_vma=False
    )
```

```python
import functools

import jax
import jax.numpy as jnp
from jax import lax
from jax.experimental import pallas as pl
from jax.experimental.pallas import tpu as pltpu
from jax.sharding import PartitionSpec as P

LANES = 128
ROW_TILE = 16
VMEM_BYTES = 64 * 1024 * 1024
MESH = pl.DeviceIdType.MESH


def round_up(value, step):
    return (value + step - 1) // step * step


def bits_of(size):
    return size.bit_length() - 1


def split_iota(shape, dim, *sizes):
    left = lax.broadcasted_iota(jnp.int32, shape, dim)
    parts = []
    for size in reversed(sizes):
        parts.append(left & (size - 1))
        left = left >> bits_of(size)
    return [left] + parts[::-1]


def one_hot(hit):
    return jnp.where(hit, 1.0, 0.0).astype(jnp.bfloat16)


def exchange_kernel(
    lam_n, pair_n, chunks, share, share_pad, rows, prows, blk,
    tiles_ref, pair_hbm, lam_hbm, count_hbm, mu_hbm, nu_hbm, occ_hbm, vir_ref,
    lhs_out, occ_wide_out, vir_rows_out,
    lhs_ref, occ_wide_ref, vir_rows_ref, out_sem,
    pair_ref, lam_ref, count_ref, mu_ref, nu_ref, occ_ref, small_sem,
    tile_buf, vir_buf, place_ref, index_ref, half_send, half_held, place_held, index_held, pick, mixed_t,
    mix_send, mix_held,
    tile_sem, vir_sem, place_ssem, place_rsem, index_ssem, index_rsem,
    half_ssem, half_rsem, mix_ssem, mix_rsem,
):
    lam_me = lax.axis_index("lam")
    pair_me = lax.axis_index("pair")
    groups = tile_buf.shape[0]
    depth = tile_buf.shape[1]
    basis = vir_buf.shape[0]
    occ_total = occ_ref.shape[0]
    both = LANES // rows
    slots = pair_ref.shape[1]
    duo = slots // groups

    barrier = pltpu.get_barrier_semaphore()
    for d in range(1, lam_n):
        pl.semaphore_signal(barrier, inc=1, device_id={"lam": lax.rem(lam_me + d, lam_n)}, device_id_type=MESH)
    for d in range(1, pair_n):
        pl.semaphore_signal(barrier, inc=1, device_id={"pair": lax.rem(pair_me + d, pair_n)}, device_id_type=MESH)

    small_copies = [
        pltpu.make_async_copy(source, target, small_sem.at[n])
        for n, (source, target) in enumerate([
            (pair_hbm, pair_ref), (lam_hbm, lam_ref), (count_hbm, count_ref),
            (mu_hbm, mu_ref), (nu_hbm, nu_ref), (occ_hbm, occ_ref),
        ])
    ]
    for copy in small_copies:
        copy.start()
    tile_copies = [
        pltpu.make_async_copy(tiles_ref.at[pl.ds(q * depth, depth)], tile_buf.at[q], tile_sem.at[q])
        for q in range(groups)
    ]
    vir_copy = pltpu.make_async_copy(vir_ref, vir_buf, vir_sem)
    for copy in tile_copies:
        copy.start()
    vir_copy.start()

    for copy in small_copies:
        copy.wait()

    slot, row_j, row_k = split_iota((slots * both * prows, LANES), 0, both, prows)
    lane_j, lane_r = split_iota((slots * both * prows, LANES), 1, rows)
    goal = jnp.zeros_like(slot)
    for t in range(slots):
        goal = jnp.where(slot == t, pair_ref[0, t], goal)
    place_ref[...] = one_hot((row_j == lane_j) & (lane_r == goal * prows + row_k))
    index_ref[...] = jnp.zeros_like(index_ref)
    index_ref[0:1, 0:rows] = mu_ref[...]
    index_ref[1:2, 0:rows] = nu_ref[...]

    lam_rows = basis // lam_n
    width = slots * prows * blk
    lane_t, _, lane_m = split_iota((1, width), 1, prows, blk)
    source = jnp.zeros_like(lane_t)
    for t in range(slots):
        first = jnp.where(count_ref[0, 0] > t, lam_ref[0, t] * blk - lam_me * lam_rows, -2 * basis)
        source = jnp.where(lane_t == t, first, source)
    source = source + lane_m
    chosen = one_hot(lax.broadcasted_iota(jnp.int32, (lam_rows, width), 0) == source)
    occ_own = occ_ref[:, pl.ds(pl.multiple_of(lam_me * lam_rows, lam_rows), lam_rows)]
    occ_tiles = jnp.dot(occ_own, chosen, preferred_element_type=jnp.float32).astype(jnp.bfloat16)
    height = lam_n * chunks * ROW_TILE
    group, _, repeat_j, _ = split_iota((height, occ_total), 0, duo, both, prows)
    repeat = one_hot(lax.broadcasted_iota(jnp.int32, (height, occ_total), 1) == group * both + repeat_j)
    factor = jnp.dot(repeat, occ_tiles, preferred_element_type=jnp.float32)
    _, row_t, _, row_k = split_iota((height, width), 0, duo, both, prows)
    lane_t, lane_k, _ = split_iota((height, width), 1, prows, blk)
    spread = jnp.where((row_t == (lane_t & (duo - 1))) & (row_k == lane_k), factor, 0.0).astype(jnp.bfloat16)

    place_copies, index_copies, mix_copies = [], [], []
    half_copies = [[] for _ in range(chunks)]

    def send_half(c, piece, begin, end):
        for d in range(1, lam_n):
            peer = lax.rem(lam_me + d, lam_n)
            copy = pltpu.make_async_remote_copy(
                src_ref=half_send.at[peer, c, pl.ds(begin, end - begin)],
                dst_ref=half_held.at[c, lam_me, pl.ds(begin, end - begin)],
                send_sem=half_ssem.at[c, piece, d], recv_sem=half_rsem.at[c, piece, d],
                device_id={"lam": peer}, device_id_type=MESH,
            )
            copy.start()
            half_copies[c].append(copy)

    early = groups // 2 * ROW_TILE
    for q in range(groups):
        tile_copies[q].wait()
        part = jnp.dot(
            spread[:, q * depth:(q + 1) * depth], tile_buf[q], preferred_element_type=jnp.float32
        ).astype(jnp.bfloat16)
        for g in range(lam_n * chunks):
            half_send[g // chunks, g % chunks, q * ROW_TILE:(q + 1) * ROW_TILE, :] = part[
                g * ROW_TILE:(g + 1) * ROW_TILE
            ]
        if (q + 1) * ROW_TILE == early:
            pl.semaphore_wait(barrier, lam_n + pair_n - 2)
            send_half(0, 0, 0, early)

    for d in range(1, lam_n):
        peer = lax.rem(lam_me + d, lam_n)
        copy = pltpu.make_async_remote_copy(
            src_ref=place_ref, dst_ref=place_held.at[lam_me],
            send_sem=place_ssem.at[d], recv_sem=place_rsem.at[d],
            device_id={"lam": peer}, device_id_type=MESH,
        )
        copy.start()
        place_copies.append(copy)
    for d in range(1, pair_n):
        peer = lax.rem(pair_me + d, pair_n)
        copy = pltpu.make_async_remote_copy(
            src_ref=index_ref, dst_ref=index_held.at[pair_me],
            send_sem=index_ssem.at[d], recv_sem=index_rsem.at[d],
            device_id={"pair": peer}, device_id_type=MESH,
        )
        copy.start()
        index_copies.append(copy)
    send_half(0, 1, early, groups * ROW_TILE)
    place_held[lam_me] = place_ref[...]
    index_held[pair_me] = index_ref[...]
    for c in range(chunks):
        half_held[c, lam_me] = half_send[lam_me, c]

    for copy in index_copies:
        copy.wait_recv()
    for p in range(pair_n):
        named = index_held[p].astype(jnp.float32)
        low = lax.broadcasted_iota(jnp.int32, (1, LANES), 1) < rows
        line = jnp.where(low, named[0:1], pltpu.roll(named, rows, 1)[1:2])
        column = jnp.transpose(jnp.broadcast_to(line, (LANES, LANES)))
        for b in range(basis // LANES):
            name = (lax.broadcasted_iota(jnp.int32, (LANES, LANES), 1) + b * LANES).astype(jnp.float32)
            hit = one_hot(column == name)
            pick[0, p * rows:(p + 1) * rows, b * LANES:(b + 1) * LANES] = hit[:rows]
            pick[1, p * rows:(p + 1) * rows, b * LANES:(b + 1) * LANES] = hit[rows:]
    occ_rows = lax.dot_general(
        pick[0], occ_ref[...], (((1,), (1,)), ((), ())), preferred_element_type=jnp.float32
    ).astype(jnp.bfloat16)
    lane_i, _ = split_iota((occ_total, occ_total * LANES), 1, LANES)
    widen = one_hot(lax.broadcasted_iota(jnp.int32, lane_i.shape, 0) == lane_i)
    occ_wide_ref[...] = jnp.dot(occ_rows, widen, preferred_element_type=jnp.float32).astype(jnp.bfloat16)
    vir_copy.wait()
    step = 2 * LANES
    for n in range(0, vir_buf.shape[1], step):
        vir_rows_ref[:, n:n + step] = jnp.dot(
            pick[1], vir_buf[:, n:n + step], preferred_element_type=jnp.float32
        ).astype(jnp.bfloat16)

    out_copies = [
        pltpu.make_async_copy(occ_wide_ref, occ_wide_out, out_sem.at[0]),
        pltpu.make_async_copy(vir_rows_ref, vir_rows_out, out_sem.at[1]),
    ]
    for copy in out_copies:
        copy.start()

    for c in range(1, chunks):
        send_half(c, 0, 0, groups * ROW_TILE)

    for copy in place_copies:
        copy.wait_recv()
    place = jnp.transpose(place_held[...].reshape(-1, LANES).astype(jnp.float32)).astype(jnp.bfloat16)

    for c in range(chunks):
        for copy in half_copies[c]:
            copy.wait_recv()
        slots = half_held[c].reshape(-1, basis)
        half_low = jnp.dot(place, slots, preferred_element_type=jnp.float32).astype(jnp.bfloat16)
        for n in range(0, vir_buf.shape[1], step):
            mixed = jnp.dot(half_low, vir_buf[:, n:n + step], preferred_element_type=jnp.float32)
            mixed_t[n:n + step, :] = jnp.transpose(mixed)
        for p in range(pair_n):
            block = mixed_t[p * share:(p + 1) * share, :]
            if share_pad > share:
                block = jnp.concatenate([block, jnp.zeros((share_pad - share, LANES), jnp.float32)], axis=0)
            mix_send[c, p] = block.astype(jnp.bfloat16)
        row_copies = []
        for d in range(1, pair_n):
            peer = lax.rem(pair_me + d, pair_n)
            copy = pltpu.make_async_remote_copy(
                src_ref=mix_send.at[c, peer], dst_ref=mix_held.at[c, pair_me],
                send_sem=mix_ssem.at[c, d], recv_sem=mix_rsem.at[c, d],
                device_id={"pair": peer}, device_id_type=MESH,
            )
            copy.start()
            row_copies.append(copy)
        mix_copies.append(row_copies)
        mix_held[c, pair_me] = mix_send[c, pair_me]

    low_lanes = lax.broadcasted_iota(jnp.int32, (share_pad, LANES), 1) < rows
    for c in range(chunks):
        for copy in mix_copies[c]:
            copy.wait_recv()
        for pp in range(pair_n // 2):
            even = mix_held[c, 2 * pp].astype(jnp.float32)
            odd = mix_held[c, 2 * pp + 1].astype(jnp.float32)
            first = jnp.where(low_lanes, even, pltpu.roll(odd, rows, 1))
            second = jnp.where(low_lanes, pltpu.roll(even, rows, 1), odd)
            lhs_ref[2 * c, :, pp * LANES:(pp + 1) * LANES] = first.astype(jnp.bfloat16)
            lhs_ref[2 * c + 1, :, pp * LANES:(pp + 1) * LANES] = second.astype(jnp.bfloat16)
        copy = pltpu.make_async_copy(
            lhs_ref.at[pl.ds(2 * c, 2)], lhs_out.at[pl.ds(2 * c, 2)], out_sem.at[2 + c]
        )
        copy.start()
        out_copies.append(copy)

    for copy in place_copies + index_copies + sum(half_copies, []) + sum(mix_copies, []):
        copy.wait_send()
    for copy in out_copies:
        copy.wait()


def product_kernel(share, lhs_ref, occ_wide_ref, vir_rows_ref, out_ref, held, sems):
    items, share_pad, total_rows = lhs_ref.shape
    vir_total = vir_rows_ref.shape[1]
    step_i = pl.program_id(0)
    last = pl.num_programs(0) - 1
    step = 2 * LANES
    middle = round_up(vir_total // 2, step)
    parts = ((0, middle), (middle, vir_total))

    def copies(at, part):
        begin, end = parts[part]
        slot = lax.rem(at, 2)
        columns = pl.ds(pl.multiple_of(at * vir_total + begin, LANES), end - begin)
        return [
            pltpu.make_async_copy(
                held.at[slot, j, :, pl.ds(begin, end - begin)], out_ref.at[j, :, columns], sems.at[slot, part, j]
            )
            for j in range(items)
        ]

    @pl.when(step_i >= 2)
    def _():
        for part in range(2):
            for copy in copies(step_i - 2, part):
                copy.wait()

    slot_now = lax.rem(step_i, 2)
    occ_wide = jnp.concatenate([occ_wide_ref[...]] * 2, axis=1)
    lhs = lhs_ref[...].reshape(items * share_pad, total_rows)
    for part in range(2):
        for n in range(*parts[part], step):
            weights = occ_wide * vir_rows_ref[:, n:n + step]
            block = jnp.dot(lhs, weights, preferred_element_type=jnp.float32)
            held[slot_now, :, :, n:n + step] = block.reshape(items, share_pad, step)[:, :share]
        for copy in copies(step_i, part):
            copy.start()

    @pl.when(step_i == last)
    def _():
        for at in (last - 1, last):
            for part in range(2):
                for copy in copies(at, part):
                    copy.wait()


def on_device(
    integrals, tile_pair, tile_lam, tile_count, mu_index, nu_index, occupied_coef, virtual_coef
):
    lam_n = lax.axis_size("lam")
    pair_n = lax.axis_size("pair")
    basis, occ_total = occupied_coef.shape
    vir_total = virtual_coef.shape[1]
    rows = mu_index.shape[0]
    slots, prows, blk = integrals.shape[1:4]
    bf16 = jnp.bfloat16
    both = LANES // rows
    occ_share = occ_total // lam_n
    chunks = occ_share // both
    share = vir_total // pair_n
    share_pad = round_up(share, ROW_TILE)
    duo = ROW_TILE // (both * prows)
    groups = slots // duo
    total_rows = rows * pair_n

    pinned = pl.BlockSpec(memory_space=pltpu.HBM)
    dma = pltpu.SemaphoreType.DMA
    chunk_rows = slots * both * prows
    lhs, occ_wide, vir_rows = pl.pallas_call(
        functools.partial(exchange_kernel, lam_n, pair_n, chunks, share, share_pad, rows, prows, blk),
        out_shape=(
            jax.ShapeDtypeStruct((occ_share, share_pad, total_rows), bf16),
            jax.ShapeDtypeStruct((total_rows, occ_total * LANES), bf16),
            jax.ShapeDtypeStruct((total_rows, vir_total), bf16),
        ),
        in_specs=[pinned] * 8,
        out_specs=(pinned, pinned, pinned),
        scratch_shapes=[
            pltpu.VMEM((occ_share, share_pad, total_rows), bf16),
            pltpu.VMEM((total_rows, occ_total * LANES), bf16),
            pltpu.VMEM((total_rows, vir_total), bf16),
            dma((2 + chunks,)),
            pltpu.SMEM((1, slots), jnp.int32),
            pltpu.SMEM((1, slots), jnp.int32),
            pltpu.SMEM((1, 1), jnp.int32),
            pltpu.VMEM((1, rows), jnp.int32),
            pltpu.VMEM((1, rows), jnp.int32),
            pltpu.VMEM((occ_total, basis), bf16),
            dma((6,)),
            pltpu.VMEM((groups, duo * prows * blk, basis), bf16),
            pltpu.VMEM((basis, vir_total), bf16),
            pltpu.VMEM((chunk_rows, LANES), bf16),
            pltpu.VMEM((8, LANES), jnp.int32),
            pltpu.VMEM((lam_n, chunks, chunk_rows, basis), bf16),
            pltpu.VMEM((chunks, lam_n, chunk_rows, basis), bf16),
            pltpu.VMEM((lam_n, chunk_rows, LANES), bf16),
            pltpu.VMEM((pair_n, 8, LANES), jnp.int32),
            pltpu.VMEM((2, total_rows, basis), bf16),
            pltpu.VMEM((vir_total, LANES), jnp.float32),
            pltpu.VMEM((chunks, pair_n, share_pad, LANES), bf16),
            pltpu.VMEM((chunks, pair_n, share_pad, LANES), bf16),
            dma((groups,)),
            dma,
            dma((lam_n,)),
            dma((lam_n,)),
            dma((pair_n,)),
            dma((pair_n,)),
            dma((chunks, 2, lam_n)),
            dma((chunks, 2, lam_n)),
            dma((chunks, pair_n)),
            dma((chunks, pair_n)),
        ],
        compiler_params=pltpu.CompilerParams(
            collective_id=0, has_side_effects=True, vmem_limit_bytes=VMEM_BYTES
        ),
        name="exchange",
    )(
        integrals.reshape(slots * prows * blk, basis), tile_pair, tile_lam, tile_count,
        mu_index[None, :], nu_index[None, :], occupied_coef.T, virtual_coef,
    )

    return pl.pallas_call(
        functools.partial(product_kernel, share),
        out_shape=jax.ShapeDtypeStruct((occ_share, share, occ_total * vir_total), jnp.float32),
        grid=(occ_total,),
        in_specs=[
            pl.BlockSpec((occ_share, share_pad, total_rows), lambda i: (0, 0, 0)),
            pl.BlockSpec((total_rows, LANES), lambda i: (0, i)),
            pl.BlockSpec((total_rows, vir_total), lambda i: (0, 0)),
        ],
        out_specs=pl.BlockSpec(memory_space=pl.ANY),
        scratch_shapes=[
            pltpu.VMEM((2, occ_share, share, vir_total), jnp.float32),
            dma((2, 2, occ_share)),
        ],
        compiler_params=pltpu.CompilerParams(vmem_limit_bytes=VMEM_BYTES),
        name="product",
    )(lhs, occ_wide, vir_rows)


def solution(mesh):
    placed = (
        P("pair", "lam", None, None, None),
        P("pair", "lam"),
        P("pair", "lam"),
        P("pair", "lam"),
        P("pair"),
        P("pair"),
        P(),
        P(),
    )
    return jax.shard_map(
        on_device, mesh=mesh, in_specs=placed, out_specs=P("lam", "pair", None), check_vma=False
    )
```
